32 devices in a mesh: dp: 16 (over z, y, core), seq: 2 (over x).
Axes of the slice: x: 2, y: 2, z: 4, core: 2. Of those that a mesh axis runs over, the one named last changes fastest.
Arguments:
- acts: bfloat16 [4096, 4096], P(('dp', 'seq')), may hold values from -6 to 6
- grad_out: bfloat16 [4096, 4096], P('dp', 'seq'), may hold values from -6 to 6
- proj_weight: bfloat16 [4096, 4096], P('dp', 'seq'), may hold values from -0.09375 to 0.09375
Outputs:
- grad_acts: float32 [4096, 4096], P(('dp', 'seq'))
- grad_weight: float32 [4096, 4096], P('dp', 'seq')
The draws below stay inside these ranges and needn't reach their ends.
All inputs are finite; a program needn't handle non-finite values.
Results may differ from the reference program's by a relative error of at most 0.014.
Values may be sent and summed in bfloat16 or wider, within the bound.
A program may use at most 128 MiB of HBM per device.

```python
import jax
import jax.numpy as jnp
from jax import lax

DI = 4096
DO = 4096
TOK_DEV = 128
TOKENS = 4096
N_DP = 16
N_SEQ = 2


def strengthened(array, rng, source, target, parts, factor):
    def block_of(position):
        return (jnp.arange(array.shape[position]) // (array.shape[position] // parts)).reshape((-1,) + (1,) * (array.ndim - 1 - position))

    one_side = jax.random.permutation(rng, parts)[block_of(target)]
    far = (block_of(target) + parts // 2) % parts
    return jnp.where((block_of(source) == one_side) | (block_of(source) == far), factor * array, array)


def steps_of(stream_key, extent, cuts, low, high):
    level, own = 1.0, jax.random.fold_in(stream_key, 6)
    for dim, shards_of in cuts:
        heights = jnp.exp(jax.random.uniform(jax.random.fold_in(own, dim), (shards_of,), jnp.float32, low / len(cuts), high / len(cuts)))
        level = level * jnp.repeat(heights, extent[dim] // shards_of).reshape([-1 if axis == dim else 1 for axis in range(len(extent))])
    return level


def noise(own_key, extent, spread, most, split=(), kind=jnp.bfloat16):
    result = spread * jax.random.normal(own_key, extent, jnp.float32)
    if split:
        result = result * steps_of(own_key, extent, split, -0.22, 0.18)
    return jnp.clip(result, -most, most).astype(kind)


def bell_draw_with(rng, extent, scale, most, pieces, heavy, held_as=jnp.bfloat16):
    entries = scale * jax.random.normal(rng, extent, jnp.float32)
    if pieces:
        entries = entries * steps_of(rng, extent, pieces, -0.22, 0.18)
    return jnp.clip(strengthened(entries, jax.random.fold_in(rng, 3), *heavy), -most, most).astype(held_as)


def setup_inputs(seed: int = 0) -> dict:
    streams_of = jax.random.split(jax.random.key(seed), 4)
    return {
        "acts": bell_draw_with(streams_of[0], (TOKENS, DI), 1.0, 6.0, ((0, 32),), (0, 1, 32, 2.75)),
        "grad_out": noise(streams_of[1], (TOKENS, DO), 1.0, 6.0, ((0, 16), (1, 2))),
        "proj_weight": noise(streams_of[2], (DI, DO), DI ** -0.5, 0.09375, ((0, 16), (1, 2))),
    }


def reference(acts, grad_out, proj_weight):
    width = DO // N_SEQ

    def add_block(index, total):
        start = (index * width).astype(jnp.int32)
        cols = lax.dynamic_slice_in_dim(grad_out, start, width, 1)
        wcols = lax.dynamic_slice_in_dim(proj_weight, start, width, 1)
        part = lax.dot_general(cols, wcols, (((1,), (1,)), ((), ())), preferred_element_type=jnp.float32)
        part = lax.optimization_barrier(part.astype(jnp.bfloat16))
        return total + part.astype(jnp.float32)
    grad_acts = lax.fori_loop(jnp.int32(0), jnp.int32(N_SEQ), add_block, jnp.zeros((TOKENS, DI), jnp.float32))
    group = TOK_DEV * N_SEQ

    def add_group(index, total):
        start = (index * group).astype(jnp.int32)
        rows_a = lax.dynamic_slice_in_dim(acts, start, group, 0)
        rows_g = lax.dynamic_slice_in_dim(grad_out, start, group, 0)
        term = lax.dot_general(rows_a, rows_g, (((0,), (0,)), ((), ())), preferred_element_type=jnp.float32)
        term = lax.optimization_barrier(term.astype(jnp.bfloat16))
        return total + term.astype(jnp.float32)
    product = lax.fori_loop(jnp.int32(0), jnp.int32(N_DP), add_group, jnp.zeros((DI, DO), jnp.float32))
    grad_weight = product / jnp.sqrt(jnp.float32(TOKENS))
    return (grad_acts, grad_weight)
```

```python
import functools

import jax
import jax.numpy as jnp
from jax import lax
from jax.experimental import pallas as pl
from jax.experimental.pallas import tpu as pltpu
from jax.sharding import PartitionSpec as P

MESH = pl.DeviceIdType.MESH
NQ = 4
PIECES = 2
BF16 = jnp.bfloat16
F32 = jnp.float32


def kernel(nz, ns, acts, go, w, ga_out, rs_out, pz_out, go_l, acts_l, wall, ga_s,
           acts_t, rr, sb, pbuf, go_send, go_recv, a_send, a_recv, ga_send, ga_recv,
           z_send, z_recv, l_sem):
    tok = acts.shape[0]
    rg, cols = go.shape
    blk = w.shape[0]
    h = blk // PIECES
    total = NQ * rg
    dp = lax.axis_index("dp")
    x = lax.axis_index("seq")
    z = dp // NQ
    q = dp % NQ
    mirror = nz - 1 - z
    pos = (z, mirror)

    def real(d, i):
        return i if d == 0 else nz - 1 - i

    def layer(qq, xx):
        return {"dp": z * NQ + qq, "seq": xx}

    def ahead(d):
        return {"dp": (z + (1 if d == 0 else -1)) * NQ + q, "seq": x}

    def part(i, size):
        return pl.ds(pl.multiple_of(i * size, size), size)

    barrier = pltpu.get_barrier_semaphore()
    for o in range(NQ * ns):
        @pl.when(o != q * ns + x)
        def _():
            pl.semaphore_signal(barrier, inc=1, device_id=layer(o // ns, o % ns), device_id_type=MESH)
    for d in range(2):
        @pl.when(pos[d] < nz - 1)
        def _():
            pl.semaphore_signal(barrier, inc=1, device_id=ahead(d), device_id_type=MESH)
    beside = (z + nz - 1) // nz + (mirror + nz - 1) // nz
    pl.semaphore_wait(barrier, NQ * ns - 1 + beside)

    def zcopy(d, t, s, src, dst):
        return pltpu.make_async_remote_copy(
            src_ref=src, dst_ref=dst, send_sem=z_send.at[d, t, s], recv_sem=z_recv.at[d, t, s],
            device_id=ahead(d), device_id_type=MESH)

    def wall_piece(i, s):
        return wall.at[pl.ds(pl.multiple_of(i * blk + s * h, h), h)]

    def rows(s):
        return pl.ds(s * h, h)

    for s in range(PIECES):
        for d in range(2):
            @pl.when(pos[d] < nz - 1)
            def _():
                zcopy(d, 0, s, w.at[rows(s)], wall_piece(z, s)).start()

    sib = q + 1 - 2 * (q % 2)
    far = (q + 2) % NQ
    sibfar = (sib + 2) % NQ

    def gcopy(k, src, slot, target):
        return pltpu.make_async_remote_copy(
            src_ref=src, dst_ref=go_l.at[part(slot, rg)], send_sem=go_send.at[k],
            recv_sem=go_recv.at[k], device_id=layer(target, x), device_id_type=MESH)

    gcopy(1, go, q, far).start()
    gcopy(0, go, q, sib).start()
    own_go = pltpu.make_async_copy(go, go_l.at[part(q, rg)], l_sem.at[0])
    own_go.start()
    own_w = pltpu.make_async_copy(w, wall.at[part(z, blk)], l_sem.at[1])
    own_w.start()
    gcopy(1, go, far, far).wait_recv()
    gcopy(2, go_l.at[part(far, rg)], far, sib).start()

    def send_acts(m):
        for o in range(NQ * ns):
            qq, xx = o // ns, o % ns
            src = acts.at[:, part(m * NQ + qq, blk)]
            dst = acts_l.at[part(q * ns + x, tok), part(m, blk)]

            @pl.when(o == q * ns + x)
            def _():
                pltpu.make_async_copy(src, dst, a_recv.at[m]).start()

            @pl.when(o != q * ns + x)
            def _():
                pltpu.make_async_remote_copy(
                    src_ref=src, dst_ref=dst, send_sem=a_send, recv_sem=a_recv.at[m],
                    device_id=layer(qq, xx), device_id_type=MESH).start()

    for t in range(1, nz):
        for d in range(2):
            @pl.when(t > pos[d])
            def _():
                send_acts(real(d, nz - t + pos[d]))
    send_acts(z)

    gcopy(0, go, sib, sib).wait_recv()
    gcopy(2, go, sibfar, sib).wait_recv()
    own_go.wait()
    own_w.wait()

    def input_grad(m):
        @pl.loop(0, NQ)
        def _(qq):
            out = lax.dot_general(
                go_l[part(qq, rg), :], wall[part(m, blk), :], (((1,), (1,)), ((), ())),
                preferred_element_type=F32)
            ga_s[part(qq, rg), part(m, blk)] = out.astype(BF16)
            for xx in range(ns):
                src = ga_s.at[part(qq * ns + xx, tok), part(m, blk)]
                dst = ga_out.at[x, :, part(m * NQ + q, blk)]
                mine = (qq * ns + xx) == (q * ns + x)

                @pl.when(mine)
                def _():
                    pltpu.make_async_copy(src, dst, ga_recv).start()

                @pl.when(jnp.logical_not(mine))
                def _():
                    pltpu.make_async_remote_copy(
                        src_ref=src, dst_ref=dst, send_sem=ga_send, recv_sem=ga_recv,
                        device_id=layer(qq, xx), device_id_type=MESH).start()

    tile = min(cols, 512)

    def weight_grad(m, slot):
        block = acts_l.at[:, part(m, blk)]
        pltpu.make_async_copy(block, block, a_recv.at[m]).wait()
        acts_t[...] = acts_l[:, part(m, blk)].T

        @pl.loop(0, cols // tile)
        def _(j):
            pbuf[slot, :, part(j, tile)] = jnp.dot(
                acts_t[...], go_l[:, part(j, tile)], preferred_element_type=F32)

    step = min(h, 32)

    def forward_sum(d, t, s):
        def emit(add):
            @pl.loop(0, h // step)
            def _(i):
                r = pl.ds(pl.multiple_of(s * h + i * step, step), step)
                value = pbuf[d, r, :]
                if add:
                    value = value + rr[d, t - 1, r, :].astype(F32)
                sb[d, t - 1, r, :] = value.astype(BF16)

        @pl.when(pos[d] > 0)
        def _():
            piece = rr.at[d, t - 1, rows(s)]
            zcopy(d, t - 1, s, piece, piece).wait_recv()
            emit(True)

        @pl.when(pos[d] == 0)
        def _():
            emit(False)

        dst = rs_out.at[d, rows(s)] if t == nz - 1 else rr.at[d, t, rows(s)]
        zcopy(d, t, s, sb.at[d, t - 1, rows(s)], dst).start()

    def pass_weight(d, t, s):
        piece = wall_piece(real(d, pos[d] - t), s)
        zcopy(d, t - 1, s, piece, piece).wait_recv()

        @pl.when(pos[d] < nz - 1)
        def _():
            zcopy(d, t, s, piece, piece).start()

    input_grad(z)
    for t in range(1, nz):
        for d in range(2):
            @pl.when(t > pos[d])
            def _():
                weight_grad(real(d, nz - t + pos[d]), d)
        for s in range(PIECES):
            for d in range(2):
                @pl.when(t <= pos[d])
                def _():
                    pass_weight(d, t, s)

                @pl.when(t > pos[d])
                def _():
                    forward_sum(d, t, s)
        for d in range(2):
            @pl.when(t <= pos[d])
            def _():
                input_grad(real(d, pos[d] - t))

    weight_grad(z, 2)
    own_p = pltpu.make_async_copy(pbuf.at[2], pz_out, l_sem.at[0])
    own_p.start()
    for d in range(2):
        @pl.when(pos[d] == 0)
        def _():
            rr[d, 0] = jnp.zeros((blk, cols), BF16)
            fill = pltpu.make_async_copy(rr.at[d, 0], rs_out.at[d], l_sem.at[1])
            fill.start()
            fill.wait()

        @pl.when(pos[d] > 0)
        def _():
            for s in range(PIECES):
                piece = rs_out.at[d, rows(s)]
                zcopy(d, nz - 1, s, piece, piece).wait_recv()

    pltpu.make_async_copy(ga_out, ga_out, ga_recv).wait()
    own_p.wait()
    for d in range(2):
        @pl.when(pos[d] < nz - 1)
        def _():
            for t in range(nz):
                for s in range(PIECES):
                    piece = sb.at[d, 0, rows(s)]
                    zcopy(d, t, s, piece, piece).wait_send()
    for k in range(3):
        gcopy(k, go, q, sib).wait_send()
    others = acts_l.at[pl.ds(0, total - tok)]
    pltpu.make_async_copy(others, others, a_send).wait()
    others = ga_s.at[pl.ds(0, total - tok)]
    pltpu.make_async_copy(others, others, ga_send).wait()


def per_device(acts, grad_out, proj_weight):
    ns = lax.axis_size("seq")
    nz = lax.axis_size("dp") // NQ
    tok, feats = acts.shape
    rg, cols = grad_out.shape
    blk = proj_weight.shape[0]
    total_tokens = tok * ns * nz * NQ
    total = NQ * rg
    anywhere = pl.BlockSpec(memory_space=pl.ANY)
    flops = 4 * total * nz * blk * cols
    parts, sums, own = pl.pallas_call(
        functools.partial(kernel, nz, ns),
        out_shape=(
            jax.ShapeDtypeStruct((ns, tok, feats), BF16),
            jax.ShapeDtypeStruct((2, blk, cols), BF16),
            jax.ShapeDtypeStruct((blk, cols), F32),
        ),
        in_specs=[anywhere] * 3,
        out_specs=(anywhere,) * 3,
        scratch_shapes=[
            pltpu.VMEM((total, cols), BF16),
            pltpu.VMEM((total, nz * blk), BF16),
            pltpu.VMEM((nz * blk, cols), BF16),
            pltpu.VMEM((total, nz * blk), BF16),
            pltpu.VMEM((blk, total), BF16),
            pltpu.VMEM((2, nz - 1, blk, cols), BF16),
            pltpu.VMEM((2, nz - 1, blk, cols), BF16),
            pltpu.VMEM((3, blk, cols), F32),
            pltpu.SemaphoreType.DMA((3,)),
            pltpu.SemaphoreType.DMA((3,)),
            pltpu.SemaphoreType.DMA,
            pltpu.SemaphoreType.DMA((nz,)),
            pltpu.SemaphoreType.DMA,
            pltpu.SemaphoreType.DMA,
            pltpu.SemaphoreType.DMA((2, nz, PIECES)),
            pltpu.SemaphoreType.DMA((2, nz, PIECES)),
            pltpu.SemaphoreType.DMA((2,)),
        ],
        compiler_params=pltpu.CompilerParams(
            collective_id=0, has_side_effects=True, vmem_limit_bytes=48 * 1024 * 1024),
        cost_estimate=pl.CostEstimate(flops=flops, bytes_accessed=16 * 1024 * 1024, transcendentals=0),
    )(acts, grad_out, proj_weight)
    grad_acts = jnp.sum(parts.astype(F32), axis=0)
    summed = own + sums[0].astype(F32) + sums[1].astype(F32)
    grad_weight = summed / jnp.sqrt(jnp.float32(total_tokens))
    return (grad_acts, grad_weight)


def solution(mesh):
    in_specs = (P(("dp", "seq"), None), P("dp", "seq"), P("dp", "seq"))
    out_specs = (P(("dp", "seq"), None), P("dp", "seq"))
    return jax.shard_map(
        per_device, mesh=mesh, in_specs=in_specs, out_specs=out_specs, check_vma=False
    )
```

```python
import functools

import jax
import jax.numpy as jnp
from jax import lax
from jax.experimental import pallas as pl
from jax.experimental.pallas import tpu as pltpu
from jax.sharding import PartitionSpec as P

MESH = pl.DeviceIdType.MESH
NQ = 4
PIECES = 4
BF16 = jnp.bfloat16
F32 = jnp.float32


def kernel(nz, ns, acts, go, w, ga_out, rs_out, pz_out, go_l, acts_l, wall, ga_s,
           acts_t, rr, sb, pbuf, own, go_send, go_recv, a_send, a_recv, ga_send, ga_recv,
           z_send, z_recv, l_sem):
    tok = acts.shape[0]
    rg, cols = go.shape
    blk = w.shape[0]
    h = blk // PIECES
    pw = cols // PIECES
    total = NQ * rg
    dp = lax.axis_index("dp")
    x = lax.axis_index("seq")
    z = dp // NQ
    q = dp % NQ
    mirror = nz - 1 - z
    pos = (z, mirror)

    def real(d, i):
        return i if d == 0 else nz - 1 - i

    def layer(qq, xx):
        return {"dp": z * NQ + qq, "seq": xx}

    def ahead(d):
        return {"dp": (z + (1 if d == 0 else -1)) * NQ + q, "seq": x}

    def part(i, size):
        return pl.ds(pl.multiple_of(i * size, size), size)

    barrier = pltpu.get_barrier_semaphore()
    for o in range(NQ * ns):
        @pl.when(o != q * ns + x)
        def _():
            pl.semaphore_signal(barrier, inc=1, device_id=layer(o // ns, o % ns), device_id_type=MESH)
    for d in range(2):
        @pl.when(pos[d] < nz - 1)
        def _():
            pl.semaphore_signal(barrier, inc=1, device_id=ahead(d), device_id_type=MESH)
    beside = (z + nz - 1) // nz + (mirror + nz - 1) // nz
    pl.semaphore_wait(barrier, NQ * ns - 1 + beside)

    def zcopy(d, t, s, src, dst):
        return pltpu.make_async_remote_copy(
            src_ref=src, dst_ref=dst, send_sem=z_send.at[d, t, s], recv_sem=z_recv.at[d, t, s],
            device_id=ahead(d), device_id_type=MESH)

    def wall_piece(i, s):
        return wall.at[pl.ds(pl.multiple_of(i * blk + s * h, h), h)]

    for s in range(PIECES):
        for d in range(2):
            @pl.when(pos[d] < nz - 1)
            def _():
                zcopy(d, 0, s, w.at[part(s, h)], wall_piece(z, s)).start()

    sib = q + 1 - 2 * (q % 2)
    far = (q + 2) % NQ
    sibfar = (sib + 2) % NQ

    def gcopy(k, s, slot, target):
        src = go.at[:, part(s, pw)] if k < 2 else go_l.at[part(slot, rg), part(s, pw)]
        return pltpu.make_async_remote_copy(
            src_ref=src, dst_ref=go_l.at[part(slot, rg), part(s, pw)], send_sem=go_send.at[k, s],
            recv_sem=go_recv.at[k, s], device_id=layer(target, x), device_id_type=MESH)

    def send_acts(m):
        @pl.loop(0, NQ * ns)
        def _(o):
            qq, xx = o // ns, o % ns
            src = acts.at[:, part(m * NQ + qq, blk)]
            dst = acts_l.at[part(q * ns + x, tok), part(m, blk)]

            @pl.when(o == q * ns + x)
            def _():
                pltpu.make_async_copy(src, dst, a_recv.at[m]).start()

            @pl.when(o != q * ns + x)
            def _():
                pltpu.make_async_remote_copy(
                    src_ref=src, dst_ref=dst, send_sem=a_send, recv_sem=a_recv.at[m],
                    device_id=layer(qq, xx), device_id_type=MESH).start()

    def send_acts_for(t):
        for d in range(2):
            @pl.when(t > pos[d])
            def _():
                send_acts(real(d, nz - t + pos[d]))

    gcopy(1, 0, q, far).start()
    gcopy(0, 0, q, sib).start()
    send_acts_for(1)
    own_go = pltpu.make_async_copy(go, go_l.at[part(q, rg)], l_sem.at[0])
    own_go.start()
    own_w = pltpu.make_async_copy(w, wall.at[part(z, blk)], l_sem.at[1])
    own_w.start()

    def gather_piece(s):
        gcopy(1, s, far, far).wait_recv()

        @pl.when(s + 1 < PIECES)
        def _():
            gcopy(1, s + 1, q, far).start()
            gcopy(0, s + 1, q, sib).start()

        gcopy(2, s, far, sib).start()

        @pl.when(s == PIECES - 1)
        def _():
            for t in range(2, nz):
                send_acts_for(t)
            send_acts(z)

        gcopy(0, s, sib, sib).wait_recv()
        gcopy(2, s, sibfar, sib).wait_recv()

        @pl.when(s == 0)
        def _():
            own_go.wait()
            own_w.wait()

    def input_grad(m):
        @pl.loop(0, NQ)
        def _(qq):
            out = lax.dot_general(
                go_l[part(qq, rg), :], wall[part(m, blk), :], (((1,), (1,)), ((), ())),
                preferred_element_type=F32)
            ga_s[part(qq, rg), part(m, blk)] = out.astype(BF16)

            @pl.loop(0, ns)
            def _(xx):
                src = ga_s.at[part(qq * ns + xx, tok), part(m, blk)]
                dst = ga_out.at[x, :, part(m * NQ + q, blk)]
                mine = (qq * ns + xx) == (q * ns + x)

                @pl.when(mine)
                def _():
                    pltpu.make_async_copy(src, dst, ga_recv).start()

                @pl.when(jnp.logical_not(mine))
                def _():
                    pltpu.make_async_remote_copy(
                        src_ref=src, dst_ref=dst, send_sem=ga_send, recv_sem=ga_recv,
                        device_id=layer(qq, xx), device_id_type=MESH).start()

    def turn_acts(m, slot):
        block = acts_l.at[:, part(m, blk)]
        pltpu.make_async_copy(block, block, a_recv.at[m]).wait()
        acts_t[slot] = acts_l[:, part(m, blk)].T

    def weight_piece(slot, s):
        return jnp.dot(acts_t[slot], go_l[:, part(s, pw)], preferred_element_type=F32)

    step = min(blk, 64)

    def forward_sum(d, t, s):
        pbuf[d] = weight_piece(d, s)

        def emit(add):
            @pl.loop(0, blk // step)
            def _(i):
                r = part(i, step)
                value = pbuf[d, r, :]
                if add:
                    value = value + rr[d, t - 1, s, r, :].astype(F32)
                sb[d, t - 1, s, r, :] = value.astype(BF16)

        @pl.when(pos[d] > 0)
        def _():
            piece = rr.at[d, t - 1, s]
            zcopy(d, t - 1, s, piece, piece).wait_recv()
            emit(True)

        @pl.when(pos[d] == 0)
        def _():
            emit(False)

        dst = rs_out.at[d, :, part(s, pw)] if t == nz - 1 else rr.at[d, t, s]
        zcopy(d, t, s, sb.at[d, t - 1, s], dst).start()

    def pass_weight(d, t, s):
        piece = wall_piece(real(d, pos[d] - t), s)
        zcopy(d, t - 1, s, piece, piece).wait_recv()

        @pl.when(pos[d] < nz - 1)
        def _():
            zcopy(d, t, s, piece, piece).start()

    for t in range(1, nz):
        @pl.loop(0, PIECES)
        def _(s):
            if t == 1:
                gather_piece(s)

            @pl.when(s == 0)
            def _():
                for d in range(2):
                    @pl.when(t > pos[d])
                    def _():
                        turn_acts(real(d, nz - t + pos[d]), d)

            for d in range(2):
                @pl.when(t <= pos[d])
                def _():
                    pass_weight(d, t, s)

                @pl.when(t > pos[d])
                def _():
                    forward_sum(d, t, s)

            if t == 1:
                @pl.when(s == PIECES - 1)
                def _():
                    input_grad(z)
            else:
                for d in range(2):
                    @pl.when((s == d) & (t - 1 <= pos[d]))
                    def _():
                        input_grad(real(d, pos[d] - (t - 1)))

    for d in range(2):
        @pl.when(nz - 1 <= pos[d])
        def _():
            input_grad(real(d, pos[d] - (nz - 1)))

    turn_acts(z, 0)

    @pl.loop(0, PIECES)
    def _(s):
        own[:, part(s, pw)] = weight_piece(0, s)

    own_p = pltpu.make_async_copy(own, pz_out, l_sem.at[0])
    own_p.start()
    for d in range(2):
        @pl.when(pos[d] == 0)
        def _():
            rr[d, 0] = jnp.zeros((PIECES, blk, pw), BF16)
            for s in range(PIECES):
                fill = pltpu.make_async_copy(rr.at[d, 0, s], rs_out.at[d, :, part(s, pw)], l_sem.at[1])
                fill.start()
                fill.wait()

        @pl.when(pos[d] > 0)
        def _():
            for s in range(PIECES):
                piece = rs_out.at[d, :, part(s, pw)]
                zcopy(d, nz - 1, s, piece, piece).wait_recv()

    pltpu.make_async_copy(ga_out, ga_out, ga_recv).wait()
    own_p.wait()
    for d in range(2):
        @pl.when(pos[d] < nz - 1)
        def _():
            for t in range(nz):
                @pl.loop(0, PIECES)
                def _(s):
                    piece = sb.at[d, 0, s]
                    zcopy(d, t, s, piece, piece).wait_send()
    for k in range(3):
        @pl.loop(0, PIECES)
        def _(s):
            gcopy(k, s, q, sib).wait_send()
    others = acts_l.at[pl.ds(0, total - tok)]
    pltpu.make_async_copy(others, others, a_send).wait()
    others = ga_s.at[pl.ds(0, total - tok)]
    pltpu.make_async_copy(others, others, ga_send).wait()


def per_device(acts, grad_out, proj_weight):
    ns = lax.axis_size("seq")
    nz = lax.axis_size("dp") // NQ
    tok, feats = acts.shape
    rg, cols = grad_out.shape
    blk = proj_weight.shape[0]
    total_tokens = tok * ns * nz * NQ
    total = NQ * rg
    anywhere = pl.BlockSpec(memory_space=pl.ANY)
    flops = 4 * total * nz * blk * cols
    parts, sums, own = pl.pallas_call(
        functools.partial(kernel, nz, ns),
        out_shape=(
            jax.ShapeDtypeStruct((ns, tok, feats), BF16),
            jax.ShapeDtypeStruct((2, blk, cols), BF16),
            jax.ShapeDtypeStruct((blk, cols), F32),
        ),
        in_specs=[anywhere] * 3,
        out_specs=(anywhere,) * 3,
        scratch_shapes=[
            pltpu.VMEM((total, cols), BF16),
            pltpu.VMEM((total, nz * blk), BF16),
            pltpu.VMEM((nz * blk, cols), BF16),
            pltpu.VMEM((total, nz * blk), BF16),
            pltpu.VMEM((2, blk, total), BF16),
            pltpu.VMEM((2, nz - 1, PIECES, blk, cols // PIECES), BF16),
            pltpu.VMEM((2, nz - 1, PIECES, blk, cols // PIECES), BF16),
            pltpu.VMEM((2, blk, cols // PIECES), F32),
            pltpu.VMEM((blk, cols), F32),
            pltpu.SemaphoreType.DMA((3, PIECES)),
            pltpu.SemaphoreType.DMA((3, PIECES)),
            pltpu.SemaphoreType.DMA,
            pltpu.SemaphoreType.DMA((nz,)),
            pltpu.SemaphoreType.DMA,
            pltpu.SemaphoreType.DMA,
            pltpu.SemaphoreType.DMA((2, nz, PIECES)),
            pltpu.SemaphoreType.DMA((2, nz, PIECES)),
            pltpu.SemaphoreType.DMA((2,)),
        ],
        compiler_params=pltpu.CompilerParams(
            collective_id=0, has_side_effects=True, vmem_limit_bytes=62 * 1024 * 1024),
        cost_estimate=pl.CostEstimate(flops=flops, bytes_accessed=16 * 1024 * 1024, transcendentals=0),
    )(acts, grad_out, proj_weight)
    grad_acts = jnp.sum(parts.astype(F32), axis=0)
    summed = own + sums[0].astype(F32) + sums[1].astype(F32)
    grad_weight = summed / jnp.sqrt(jnp.float32(total_tokens))
    return (grad_acts, grad_weight)


def solution(mesh):
    in_specs = (P(("dp", "seq"), None), P("dp", "seq"), P("dp", "seq"))
    out_specs = (P(("dp", "seq"), None), P("dp", "seq"))
    return jax.shard_map(
        per_device, mesh=mesh, in_specs=in_specs, out_specs=out_specs, check_vma=False
    )
```

```python
import functools

import jax
import jax.numpy as jnp
from jax import lax
from jax.experimental import pallas as pl
from jax.experimental.pallas import tpu as pltpu
from jax.sharding import PartitionSpec as P

MESH = pl.DeviceIdType.MESH
NQ = 4
PIECES = 4
BF16 = jnp.bfloat16
F32 = jnp.float32


def kernel(nz, ns, acts, go, w, ga_out, rs_out, pz_out, go_l, acts_l, wall, ga_s,
           acts_t, rr, sb, pbuf, own, go_send, go_recv, a_send, a_recv, ga_send, ga_recv,
           z_send, z_recv, l_sem):
    tok = acts.shape[0]
    rg, cols = go.shape
    blk = w.shape[0]
    h = blk // PIECES
    pw = cols // PIECES
    total = NQ * rg
    dp = lax.axis_index("dp")
    x = lax.axis_index("seq")
    z = dp // NQ
    q = dp % NQ
    mirror = nz - 1 - z
    pos = (z, mirror)

    def real(d, i):
        return i if d == 0 else nz - 1 - i

    def layer(qq, xx):
        return {"dp": z * NQ + qq, "seq": xx}

    def ahead(d):
        return {"dp": (z + (1 if d == 0 else -1)) * NQ + q, "seq": x}

    def part(i, size):
        return pl.ds(pl.multiple_of(i * size, size), size)

    barrier = pltpu.get_barrier_semaphore()
    for o in range(NQ * ns):
        @pl.when(o != q * ns + x)
        def _():
            pl.semaphore_signal(barrier, inc=1, device_id=layer(o // ns, o % ns), device_id_type=MESH)
    for d in range(2):
        @pl.when(pos[d] < nz - 1)
        def _():
            pl.semaphore_signal(barrier, inc=1, device_id=ahead(d), device_id_type=MESH)
    beside = (z + nz - 1) // nz + (mirror + nz - 1) // nz
    pl.semaphore_wait(barrier, NQ * ns - 1 + beside)

    def zcopy(d, t, s, src, dst):
        return pltpu.make_async_remote_copy(
            src_ref=src, dst_ref=dst, send_sem=z_send.at[d, t, s], recv_sem=z_recv.at[d, t, s],
            device_id=ahead(d), device_id_type=MESH)

    def wall_piece(i, s):
        return wall.at[pl.ds(pl.multiple_of(i * blk + s * h, h), h)]

    for s in range(PIECES):
        for d in range(2):
            @pl.when(pos[d] < nz - 1)
            def _():
                zcopy(d, 0, s, w.at[part(s, h)], wall_piece(z, s)).start()

    sib = q + 1 - 2 * (q % 2)
    far = (q + 2) % NQ
    sibfar = (sib + 2) % NQ

    def gcopy(k, s, slot, target):
        src = go.at[:, part(s, pw)] if k < 2 else go_l.at[part(slot, rg), part(s, pw)]
        return pltpu.make_async_remote_copy(
            src_ref=src, dst_ref=go_l.at[part(slot, rg), part(s, pw)], send_sem=go_send.at[k, s],
            recv_sem=go_recv.at[k, s], device_id=layer(target, x), device_id_type=MESH)

    def send_acts(m):
        @pl.loop(0, NQ * ns)
        def _(o):
            qq, xx = o // ns, o % ns
            src = acts.at[:, part(m * NQ + qq, blk)]
            dst = acts_l.at[part(q * ns + x, tok), part(m, blk)]

            @pl.when(o == q * ns + x)
            def _():
                pltpu.make_async_copy(src, dst, a_recv.at[m]).start()

            @pl.when(o != q * ns + x)
            def _():
                pltpu.make_async_remote_copy(
                    src_ref=src, dst_ref=dst, send_sem=a_send, recv_sem=a_recv.at[m],
                    device_id=layer(qq, xx), device_id_type=MESH).start()

    def send_acts_for(t):
        for d in range(2):
            @pl.when(t > pos[d])
            def _():
                send_acts(real(d, nz - t + pos[d]))

    gcopy(1, 0, q, far).start()
    gcopy(0, 0, q, sib).start()
    send_acts_for(1)
    gcopy(1, 1, q, far).start()
    gcopy(0, 1, q, sib).start()
    own_go = pltpu.make_async_copy(go, go_l.at[part(q, rg)], l_sem.at[0])
    own_go.start()
    own_w = pltpu.make_async_copy(w, wall.at[part(z, blk)], l_sem.at[1])
    own_w.start()

    def gather_piece(s):
        gcopy(1, s, far, far).wait_recv()

        gcopy(2, s, far, sib).start()

        @pl.when(s + 2 < PIECES)
        def _():
            gcopy(1, s + 2, q, far).start()
            gcopy(0, s + 2, q, sib).start()

        @pl.when(s == PIECES - 2)
        def _():
            send_acts_for(2)

        @pl.when(s == PIECES - 1)
        def _():
            for t in range(3, nz):
                send_acts_for(t)
            send_acts(z)

        gcopy(0, s, sib, sib).wait_recv()
        gcopy(2, s, sibfar, sib).wait_recv()

        @pl.when(s == 0)
        def _():
            own_go.wait()
            own_w.wait()

    def input_grad(m):
        @pl.loop(0, NQ)
        def _(qq):
            out = lax.dot_general(
                go_l[part(qq, rg), :], wall[part(m, blk), :], (((1,), (1,)), ((), ())),
                preferred_element_type=F32)
            ga_s[part(qq, rg), part(m, blk)] = out.astype(BF16)

            @pl.loop(0, ns)
            def _(xx):
                src = ga_s.at[part(qq * ns + xx, tok), part(m, blk)]
                dst = ga_out.at[x, :, part(m * NQ + q, blk)]
                mine = (qq * ns + xx) == (q * ns + x)

                @pl.when(mine)
                def _():
                    pltpu.make_async_copy(src, dst, ga_recv).start()

                @pl.when(jnp.logical_not(mine))
                def _():
                    pltpu.make_async_remote_copy(
                        src_ref=src, dst_ref=dst, send_sem=ga_send, recv_sem=ga_recv,
                        device_id=layer(qq, xx), device_id_type=MESH).start()

    def turn_acts(m, slot):
        block = acts_l.at[:, part(m, blk)]
        pltpu.make_async_copy(block, block, a_recv.at[m]).wait()
        acts_t[slot] = acts_l[:, part(m, blk)].T

    def weight_piece(slot, s):
        return jnp.dot(acts_t[slot], go_l[:, part(s, pw)], preferred_element_type=F32)

    step = min(blk, 64)

    def forward_sum(d, t, s):
        pbuf[d] = weight_piece(d, s)

        def emit(add):
            @pl.loop(0, blk // step)
            def _(i):
                r = part(i, step)
                value = pbuf[d, r, :]
                if add:
                    value = value + rr[d, t - 1, s, r, :].astype(F32)
                sb[d, t - 1, s, r, :] = value.astype(BF16)

        @pl.when(pos[d] > 0)
        def _():
            piece = rr.at[d, t - 1, s]
            zcopy(d, t - 1, s, piece, piece).wait_recv()
            emit(True)

        @pl.when(pos[d] == 0)
        def _():
            emit(False)

        dst = rs_out.at[d, :, part(s, pw)] if t == nz - 1 else rr.at[d, t, s]
        zcopy(d, t, s, sb.at[d, t - 1, s], dst).start()

    def pass_weight(d, t, s):
        piece = wall_piece(real(d, pos[d] - t), s)
        zcopy(d, t - 1, s, piece, piece).wait_recv()

        @pl.when(pos[d] < nz - 1)
        def _():
            zcopy(d, t, s, piece, piece).start()

    for t in range(1, nz):
        @pl.loop(0, PIECES)
        def _(s):
            if t == 1:
                gather_piece(s)

            @pl.when(s == 0)
            def _():
                for d in range(2):
                    @pl.when(t > pos[d])
                    def _():
                        turn_acts(real(d, nz - t + pos[d]), d)

            for d in range(2):
                @pl.when(t <= pos[d])
                def _():
                    pass_weight(d, t, s)

                @pl.when(t > pos[d])
                def _():
                    forward_sum(d, t, s)

            if t == 1:
                @pl.when(s == PIECES - 1)
                def _():
                    input_grad(z)
            else:
                for d in range(2):
                    @pl.when((s == d) & (t - 1 <= pos[d]))
                    def _():
                        input_grad(real(d, pos[d] - (t - 1)))

    for d in range(2):
        @pl.when(nz - 1 <= pos[d])
        def _():
            input_grad(real(d, pos[d] - (nz - 1)))

    turn_acts(z, 0)

    @pl.loop(0, PIECES)
    def _(s):
        own[:, part(s, pw)] = weight_piece(0, s)

    own_p = pltpu.make_async_copy(own, pz_out, l_sem.at[0])
    own_p.start()
    for d in range(2):
        @pl.when(pos[d] == 0)
        def _():
            rr[d, 0] = jnp.zeros((PIECES, blk, pw), BF16)
            for s in range(PIECES):
                fill = pltpu.make_async_copy(rr.at[d, 0, s], rs_out.at[d, :, part(s, pw)], l_sem.at[1])
                fill.start()
                fill.wait()

        @pl.when(pos[d] > 0)
        def _():
            for s in range(PIECES):
                piece = rs_out.at[d, :, part(s, pw)]
                zcopy(d, nz - 1, s, piece, piece).wait_recv()

    pltpu.make_async_copy(ga_out, ga_out, ga_recv).wait()
    own_p.wait()
    for d in range(2):
        @pl.when(pos[d] < nz - 1)
        def _():
            for t in range(nz):
                @pl.loop(0, PIECES)
                def _(s):
                    piece = sb.at[d, 0, s]
                    zcopy(d, t, s, piece, piece).wait_send()
    for k in range(3):
        @pl.loop(0, PIECES)
        def _(s):
            gcopy(k, s, q, sib).wait_send()
    others = acts_l.at[pl.ds(0, total - tok)]
    pltpu.make_async_copy(others, others, a_send).wait()
    others = ga_s.at[pl.ds(0, total - tok)]
    pltpu.make_async_copy(others, others, ga_send).wait()


def per_device(acts, grad_out, proj_weight):
    ns = lax.axis_size("seq")
    nz = lax.axis_size("dp") // NQ
    tok, feats = acts.shape
    rg, cols = grad_out.shape
    blk = proj_weight.shape[0]
    total_tokens = tok * ns * nz * NQ
    total = NQ * rg
    anywhere = pl.BlockSpec(memory_space=pl.ANY)
    flops = 4 * total * nz * blk * cols
    parts, sums, own = pl.pallas_call(
        functools.partial(kernel, nz, ns),
        out_shape=(
            jax.ShapeDtypeStruct((ns, tok, feats), BF16),
            jax.ShapeDtypeStruct((2, blk, cols), BF16),
            jax.ShapeDtypeStruct((blk, cols), F32),
        ),
        in_specs=[anywhere] * 3,
        out_specs=(anywhere,) * 3,
        scratch_shapes=[
            pltpu.VMEM((total, cols), BF16),
            pltpu.VMEM((total, nz * blk), BF16),
            pltpu.VMEM((nz * blk, cols), BF16),
            pltpu.VMEM((total, nz * blk), BF16),
            pltpu.VMEM((2, blk, total), BF16),
            pltpu.VMEM((2, nz - 1, PIECES, blk, cols // PIECES), BF16),
            pltpu.VMEM((2, nz - 1, PIECES, blk, cols // PIECES), BF16),
            pltpu.VMEM((2, blk, cols // PIECES), F32),
            pltpu.VMEM((blk, cols), F32),
            pltpu.SemaphoreType.DMA((3, PIECES)),
            pltpu.SemaphoreType.DMA((3, PIECES)),
            pltpu.SemaphoreType.DMA,
            pltpu.SemaphoreType.DMA((nz,)),
            pltpu.SemaphoreType.DMA,
            pltpu.SemaphoreType.DMA,
            pltpu.SemaphoreType.DMA((2, nz, PIECES)),
            pltpu.SemaphoreType.DMA((2, nz, PIECES)),
            pltpu.SemaphoreType.DMA((2,)),
        ],
        compiler_params=pltpu.CompilerParams(
            collective_id=0, has_side_effects=True, vmem_limit_bytes=40 * 1024 * 1024),
        cost_estimate=pl.CostEstimate(flops=flops, bytes_accessed=16 * 1024 * 1024, transcendentals=0),
    )(*[pltpu.with_memory_space_constraint(a, pltpu.HBM) for a in (acts, grad_out, proj_weight)])
    grad_acts = jnp.sum(parts.astype(F32), axis=0)
    summed = own + sums[0].astype(F32) + sums[1].astype(F32)
    grad_weight = summed / jnp.sqrt(jnp.float32(total_tokens))
    return (grad_acts, grad_weight)


def solution(mesh):
    in_specs = (P(("dp", "seq"), None), P("dp", "seq"), P("dp", "seq"))
    out_specs = (P(("dp", "seq"), None), P("dp", "seq"))
    return jax.shard_map(
        per_device, mesh=mesh, in_specs=in_specs, out_specs=out_specs, check_vma=False
    )
```

```python
import functools

import jax
import jax.numpy as jnp
from jax import lax
from jax.experimental import pallas as pl
from jax.experimental.pallas import tpu as pltpu
from jax.sharding import PartitionSpec as P

MESH = pl.DeviceIdType.MESH
NQ = 4
PIECES = 4
BF16 = jnp.bfloat16
F32 = jnp.float32


def kernel(nz, ns, acts, go, w, ga_out, rs_out, pz_out, go_l, acts_l, wall, ga_s,
           acts_t, rr, sb, pbuf, own, go_send, go_recv, a_send, a_recv, ga_send, ga_recv,
           z_send, z_recv, l_sem):
    tok = acts.shape[0]
    rg, cols = go.shape
    blk = w.shape[0]
    h = blk // PIECES
    pw = cols // PIECES
    total = NQ * rg
    dp = lax.axis_index("dp")
    x = lax.axis_index("seq")
    z = dp // NQ
    q = dp % NQ
    mirror = nz - 1 - z
    pos = (z, mirror)

    def real(d, i):
        return i if d == 0 else nz - 1 - i

    def layer(qq, xx):
        return {"dp": z * NQ + qq, "seq": xx}

    def ahead(d):
        return {"dp": (z + (1 if d == 0 else -1)) * NQ + q, "seq": x}

    def part(i, size):
        return pl.ds(pl.multiple_of(i * size, size), size)

    barrier = pltpu.get_barrier_semaphore()
    for o in range(NQ * ns):
        @pl.when(o != q * ns + x)
        def _():
            pl.semaphore_signal(barrier, inc=1, device_id=layer(o // ns, o % ns), device_id_type=MESH)
    for d in range(2):
        @pl.when(pos[d] < nz - 1)
        def _():
            pl.semaphore_signal(barrier, inc=1, device_id=ahead(d), device_id_type=MESH)
    beside = (z + nz - 1) // nz + (mirror + nz - 1) // nz
    pl.semaphore_wait(barrier, NQ * ns - 1 + beside)

    def zcopy(d, t, s, src, dst):
        return pltpu.make_async_remote_copy(
            src_ref=src, dst_ref=dst, send_sem=z_send.at[d, t, s], recv_sem=z_recv.at[d, t, s],
            device_id=ahead(d), device_id_type=MESH)

    def wall_piece(i, s):
        return wall.at[pl.ds(pl.multiple_of(i * blk + s * h, h), h)]

    def send_weight(s):
        for d in range(2):
            @pl.when(pos[d] < nz - 1)
            def _():
                zcopy(d, 0, s, w.at[part(s, h)], wall_piece(z, s)).start()

    sib = q + 1 - 2 * (q % 2)
    far = (q + 2) % NQ
    sibfar = (sib + 2) % NQ

    def gcopy(k, s, slot, target):
        src = go.at[:, part(s, pw)] if k < 2 else go_l.at[part(slot, rg), part(s, pw)]
        return pltpu.make_async_remote_copy(
            src_ref=src, dst_ref=go_l.at[part(slot, rg), part(s, pw)], send_sem=go_send.at[k, s],
            recv_sem=go_recv.at[k, s], device_id=layer(target, x), device_id_type=MESH)

    def send_acts(m):
        @pl.loop(0, NQ * ns)
        def _(o):
            qq, xx = o // ns, o % ns
            src = acts.at[:, part(m * NQ + qq, blk)]
            dst = acts_l.at[part(q * ns + x, tok), part(m, blk)]

            @pl.when(o == q * ns + x)
            def _():
                pltpu.make_async_copy(src, dst, a_recv.at[m]).start()

            @pl.when(o != q * ns + x)
            def _():
                pltpu.make_async_remote_copy(
                    src_ref=src, dst_ref=dst, send_sem=a_send, recv_sem=a_recv.at[m],
                    device_id=layer(qq, xx), device_id_type=MESH).start()

    def send_acts_for(t):
        for d in range(2):
            @pl.when(t > pos[d])
            def _():
                send_acts(real(d, nz - t + pos[d]))

    gcopy(1, 0, q, far).start()
    gcopy(0, 0, q, sib).start()
    send_weight(0)
    send_acts_for(1)
    send_weight(1)
    gcopy(1, 1, q, far).start()
    gcopy(0, 1, q, sib).start()
    own_go = pltpu.make_async_copy(go, go_l.at[part(q, rg)], l_sem.at[0])
    own_go.start()
    own_w = pltpu.make_async_copy(w, wall.at[part(z, blk)], l_sem.at[1])
    own_w.start()

    def gather_piece(s):
        gcopy(1, s, far, far).wait_recv()

        gcopy(2, s, far, sib).start()

        @pl.when(s + 2 < PIECES)
        def _():
            gcopy(1, s + 2, q, far).start()
            gcopy(0, s + 2, q, sib).start()
            send_weight(s + 2)

        @pl.when(s == PIECES - 2)
        def _():
            send_acts_for(2)

        @pl.when(s == PIECES - 1)
        def _():
            for t in range(3, nz):
                send_acts_for(t)
            send_acts(z)

        gcopy(0, s, sib, sib).wait_recv()
        gcopy(2, s, sibfar, sib).wait_recv()

        @pl.when(s == 0)
        def _():
            own_go.wait()
            own_w.wait()

    def input_grad(m):
        @pl.loop(0, NQ)
        def _(qq):
            out = lax.dot_general(
                go_l[part(qq, rg), :], wall[part(m, blk), :], (((1,), (1,)), ((), ())),
                preferred_element_type=F32)
            ga_s[part(qq, rg), part(m, blk)] = out.astype(BF16)

            @pl.loop(0, ns)
            def _(xx):
                src = ga_s.at[part(qq * ns + xx, tok), part(m, blk)]
                dst = ga_out.at[x, :, part(m * NQ + q, blk)]
                mine = (qq * ns + xx) == (q * ns + x)

                @pl.when(mine)
                def _():
                    pltpu.make_async_copy(src, dst, ga_recv).start()

                @pl.when(jnp.logical_not(mine))
                def _():
                    pltpu.make_async_remote_copy(
                        src_ref=src, dst_ref=dst, send_sem=ga_send, recv_sem=ga_recv,
                        device_id=layer(qq, xx), device_id_type=MESH).start()

    def turn_acts(m, slot):
        block = acts_l.at[:, part(m, blk)]
        pltpu.make_async_copy(block, block, a_recv.at[m]).wait()
        acts_t[slot] = acts_l[:, part(m, blk)].T

    def weight_piece(slot, s):
        return jnp.dot(acts_t[slot], go_l[:, part(s, pw)], preferred_element_type=F32)

    step = min(blk, 64)

    def forward_sum(d, t, s):
        pbuf[d] = weight_piece(d, s)

        def emit(add):
            @pl.loop(0, blk // step)
            def _(i):
                r = part(i, step)
                value = pbuf[d, r, :]
                if add:
                    value = value + rr[d, t - 1, s, r, :].astype(F32)
                sb[d, t - 1, s, r, :] = value.astype(BF16)

        @pl.when(pos[d] > 0)
        def _():
            piece = rr.at[d, t - 1, s]
            zcopy(d, t - 1, s, piece, piece).wait_recv()
            emit(True)

        @pl.when(pos[d] == 0)
        def _():
            emit(False)

        dst = rs_out.at[d, :, part(s, pw)] if t == nz - 1 else rr.at[d, t, s]
        zcopy(d, t, s, sb.at[d, t - 1, s], dst).start()

    def pass_weight(d, t, s):
        piece = wall_piece(real(d, pos[d] - t), s)
        zcopy(d, t - 1, s, piece, piece).wait_recv()

        @pl.when(pos[d] < nz - 1)
        def _():
            zcopy(d, t, s, piece, piece).start()

    for t in range(1, nz):
        @pl.loop(0, PIECES)
        def _(s):
            if t == 1:
                gather_piece(s)

            @pl.when(s == 0)
            def _():
                for d in range(2):
                    @pl.when(t > pos[d])
                    def _():
                        turn_acts(real(d, nz - t + pos[d]), d)

            for d in range(2):
                @pl.when(t <= pos[d])
                def _():
                    pass_weight(d, t, s)

                @pl.when(t > pos[d])
                def _():
                    forward_sum(d, t, s)

            if t == 1:
                @pl.when(s == PIECES - 1)
                def _():
                    input_grad(z)
            else:
                for d in range(2):
                    @pl.when((s == d) & (t - 1 <= pos[d]))
                    def _():
                        input_grad(real(d, pos[d] - (t - 1)))

    for d in range(2):
        @pl.when(nz - 1 <= pos[d])
        def _():
            input_grad(real(d, pos[d] - (nz - 1)))

    turn_acts(z, 0)

    @pl.loop(0, PIECES)
    def _(s):
        own[:, part(s, pw)] = weight_piece(0, s)

    own_p = pltpu.make_async_copy(own, pz_out, l_sem.at[0])
    own_p.start()
    for d in range(2):
        @pl.when(pos[d] == 0)
        def _():
            rr[d, 0] = jnp.zeros((PIECES, blk, pw), BF16)
            for s in range(PIECES):
                fill = pltpu.make_async_copy(rr.at[d, 0, s], rs_out.at[d, :, part(s, pw)], l_sem.at[1])
                fill.start()
                fill.wait()

        @pl.when(pos[d] > 0)
        def _():
            for s in range(PIECES):
                piece = rs_out.at[d, :, part(s, pw)]
                zcopy(d, nz - 1, s, piece, piece).wait_recv()

    pltpu.make_async_copy(ga_out, ga_out, ga_recv).wait()
    own_p.wait()
    for d in range(2):
        @pl.when(pos[d] < nz - 1)
        def _():
            for t in range(nz):
                @pl.loop(0, PIECES)
                def _(s):
                    piece = sb.at[d, 0, s]
                    zcopy(d, t, s, piece, piece).wait_send()
    for k in range(3):
        @pl.loop(0, PIECES)
        def _(s):
            gcopy(k, s, q, sib).wait_send()
    others = acts_l.at[pl.ds(0, total - tok)]
    pltpu.make_async_copy(others, others, a_send).wait()
    others = ga_s.at[pl.ds(0, total - tok)]
    pltpu.make_async_copy(others, others, ga_send).wait()


def per_device(acts, grad_out, proj_weight):
    ns = lax.axis_size("seq")
    nz = lax.axis_size("dp") // NQ
    tok, feats = acts.shape
    rg, cols = grad_out.shape
    blk = proj_weight.shape[0]
    total_tokens = tok * ns * nz * NQ
    total = NQ * rg
    anywhere = pl.BlockSpec(memory_space=pl.ANY)
    flops = 4 * total * nz * blk * cols
    parts, sums, own = pl.pallas_call(
        functools.partial(kernel, nz, ns),
        out_shape=(
            jax.ShapeDtypeStruct((ns, tok, feats), BF16),
            jax.ShapeDtypeStruct((2, blk, cols), BF16),
            jax.ShapeDtypeStruct((blk, cols), F32),
        ),
        in_specs=[anywhere] * 3,
        out_specs=(anywhere,) * 3,
        scratch_shapes=[
            pltpu.VMEM((total, cols), BF16),
            pltpu.VMEM((total, nz * blk), BF16),
            pltpu.VMEM((nz * blk, cols), BF16),
            pltpu.VMEM((total, nz * blk), BF16),
            pltpu.VMEM((2, blk, total), BF16),
            pltpu.VMEM((2, nz - 1, PIECES, blk, cols // PIECES), BF16),
            pltpu.VMEM((2, nz - 1, PIECES, blk, cols // PIECES), BF16),
            pltpu.VMEM((2, blk, cols // PIECES), F32),
            pltpu.VMEM((blk, cols), F32),
            pltpu.SemaphoreType.DMA((3, PIECES)),
            pltpu.SemaphoreType.DMA((3, PIECES)),
            pltpu.SemaphoreType.DMA,
            pltpu.SemaphoreType.DMA((nz,)),
            pltpu.SemaphoreType.DMA,
            pltpu.SemaphoreType.DMA,
            pltpu.SemaphoreType.DMA((2, nz, PIECES)),
            pltpu.SemaphoreType.DMA((2, nz, PIECES)),
            pltpu.SemaphoreType.DMA((2,)),
        ],
        compiler_params=pltpu.CompilerParams(
            collective_id=0, has_side_effects=True, vmem_limit_bytes=40 * 1024 * 1024),
        cost_estimate=pl.CostEstimate(flops=flops, bytes_accessed=16 * 1024 * 1024, transcendentals=0),
    )(*[pltpu.with_memory_space_constraint(a, pltpu.HBM) for a in (acts, grad_out, proj_weight)])
    grad_acts = jnp.sum(parts.astype(F32), axis=0)
    summed = own + sums[0].astype(F32) + sums[1].astype(F32)
    grad_weight = summed / jnp.sqrt(jnp.float32(total_tokens))
    return (grad_acts, grad_weight)


def solution(mesh):
    in_specs = (P(("dp", "seq"), None), P("dp", "seq"), P("dp", "seq"))
    out_specs = (P(("dp", "seq"), None), P("dp", "seq"))
    return jax.shard_map(
        per_device, mesh=mesh, in_specs=in_specs, out_specs=out_specs, check_vma=False
    )
```

```python
import functools

import jax
import jax.numpy as jnp
from jax import lax
from jax.experimental import pallas as pl
from jax.experimental.pallas import tpu as pltpu
from jax.sharding import PartitionSpec as P

MESH = pl.DeviceIdType.MESH
NQ = 4
BF16 = jnp.bfloat16
F32 = jnp.float32


def kernel(nz, ns, pieces, acts, go, w, ga_out, rs_out, pz_out, go_l, acts_l, wall, ga_s,
           acts_t, rr, sb, pbuf, own, go_send, go_recv, a_send, a_recv, ga_send, ga_recv,
           z_send, z_recv, l_sem):
    tok = acts.shape[0]
    rg, cols = go.shape
    blk = w.shape[0]
    h = blk // pieces
    pw = cols // pieces
    total = NQ * rg
    dp = lax.axis_index("dp")
    x = lax.axis_index("seq")
    z = dp // NQ
    q = dp % NQ
    mirror = nz - 1 - z
    pos = (z, mirror)

    def real(d, i):
        return i if d == 0 else nz - 1 - i

    def layer(qq, xx):
        return {"dp": z * NQ + qq, "seq": xx}

    def ahead(d):
        return {"dp": (z + (1 if d == 0 else -1)) * NQ + q, "seq": x}

    def part(i, size):
        return pl.ds(pl.multiple_of(i * size, size), size)

    barrier = pltpu.get_barrier_semaphore()
    for o in range(NQ * ns):
        @pl.when(o != q * ns + x)
        def _():
            pl.semaphore_signal(barrier, inc=1, device_id=layer(o // ns, o % ns), device_id_type=MESH)
    for d in range(2):
        @pl.when(pos[d] < nz - 1)
        def _():
            pl.semaphore_signal(barrier, inc=1, device_id=ahead(d), device_id_type=MESH)
    beside = (z + nz - 1) // nz + (mirror + nz - 1) // nz
    pl.semaphore_wait(barrier, NQ * ns - 1 + beside)

    def zcopy(d, t, s, src, dst):
        return pltpu.make_async_remote_copy(
            src_ref=src, dst_ref=dst, send_sem=z_send.at[d, t, s], recv_sem=z_recv.at[d, t, s],
            device_id=ahead(d), device_id_type=MESH)

    def wall_piece(i, s):
        return wall.at[pl.ds(pl.multiple_of(i * blk + s * h, h), h)]

    def send_weight(s):
        for d in range(2):
            @pl.when(pos[d] < nz - 1)
            def _():
                zcopy(d, 0, s, w.at[part(s, h)], wall_piece(z, s)).start()

    sib = q + 1 - 2 * (q % 2)
    far = (q + 2) % NQ
    sibfar = (sib + 2) % NQ

    def gcopy(k, s, slot, target):
        src = go.at[:, part(s, pw)] if k < 2 else go_l.at[part(slot, rg), part(s, pw)]
        return pltpu.make_async_remote_copy(
            src_ref=src, dst_ref=go_l.at[part(slot, rg), part(s, pw)], send_sem=go_send.at[k, s],
            recv_sem=go_recv.at[k, s], device_id=layer(target, x), device_id_type=MESH)

    def send_acts(m):
        @pl.loop(0, NQ * ns)
        def _(o):
            qq, xx = o // ns, o % ns
            src = acts.at[:, part(m * NQ + qq, blk)]
            dst = acts_l.at[part(q * ns + x, tok), part(m, blk)]

            @pl.when(o == q * ns + x)
            def _():
                pltpu.make_async_copy(src, dst, a_recv.at[m]).start()

            @pl.when(o != q * ns + x)
            def _():
                pltpu.make_async_remote_copy(
                    src_ref=src, dst_ref=dst, send_sem=a_send, recv_sem=a_recv.at[m],
                    device_id=layer(qq, xx), device_id_type=MESH).start()

    def send_acts_for(t):
        for d in range(2):
            @pl.when(t > pos[d])
            def _():
                send_acts(real(d, nz - t + pos[d]))

    gcopy(1, 0, q, far).start()
    gcopy(0, 0, q, sib).start()
    send_weight(0)
    send_acts_for(1)
    send_weight(1)
    gcopy(1, 1, q, far).start()
    gcopy(0, 1, q, sib).start()
    own_go = pltpu.make_async_copy(go, go_l.at[part(q, rg)], l_sem.at[0])
    own_go.start()
    own_w = pltpu.make_async_copy(w, wall.at[part(z, blk)], l_sem.at[1])
    own_w.start()

    def gather_piece(s):
        gcopy(1, s, far, far).wait_recv()

        gcopy(2, s, far, sib).start()

        @pl.when(s + 2 < pieces)
        def _():
            gcopy(1, s + 2, q, far).start()
            gcopy(0, s + 2, q, sib).start()
            send_weight(s + 2)

        @pl.when(s == pieces - 2)
        def _():
            send_acts_for(2)

        @pl.when(s == pieces - 1)
        def _():
            for t in range(3, nz):
                send_acts_for(t)
            send_acts(z)

        gcopy(0, s, sib, sib).wait_recv()
        gcopy(2, s, sibfar, sib).wait_recv()

        @pl.when(s == 0)
        def _():
            own_go.wait()
            own_w.wait()

    def input_grad(m):
        @pl.loop(0, NQ)
        def _(qq):
            out = lax.dot_general(
                go_l[part(qq, rg), :], wall[part(m, blk), :], (((1,), (1,)), ((), ())),
                preferred_element_type=F32)
            ga_s[part(qq, rg), part(m, blk)] = out.astype(BF16)

            @pl.loop(0, ns)
            def _(xx):
                src = ga_s.at[part(qq * ns + xx, tok), part(m, blk)]
                dst = ga_out.at[x, :, part(m * NQ + q, blk)]
                mine = (qq * ns + xx) == (q * ns + x)

                @pl.when(mine)
                def _():
                    pltpu.make_async_copy(src, dst, ga_recv).start()

                @pl.when(jnp.logical_not(mine))
                def _():
                    pltpu.make_async_remote_copy(
                        src_ref=src, dst_ref=dst, send_sem=ga_send, recv_sem=ga_recv,
                        device_id=layer(qq, xx), device_id_type=MESH).start()

    def turn_acts(m, slot):
        block = acts_l.at[:, part(m, blk)]
        pltpu.make_async_copy(block, block, a_recv.at[m]).wait()
        acts_t[slot] = acts_l[:, part(m, blk)].T

    def weight_piece(slot, s):
        return jnp.dot(acts_t[slot], go_l[:, part(s, pw)], preferred_element_type=F32)

    step = min(blk, 64)

    def forward_sum(d, t, s):
        pbuf[d] = weight_piece(d, s)

        def emit(add):
            @pl.loop(0, blk // step)
            def _(i):
                r = part(i, step)
                value = pbuf[d, r, :]
                if add:
                    value = value + rr[d, t - 1, s, r, :].astype(F32)
                sb[d, t - 1, s, r, :] = value.astype(BF16)

        @pl.when(pos[d] > 0)
        def _():
            piece = rr.at[d, t - 1, s]
            zcopy(d, t - 1, s, piece, piece).wait_recv()
            emit(True)

        @pl.when(pos[d] == 0)
        def _():
            emit(False)

        dst = rs_out.at[d, :, part(s, pw)] if t == nz - 1 else rr.at[d, t, s]
        zcopy(d, t, s, sb.at[d, t - 1, s], dst).start()

    def pass_weight(d, t, s):
        piece = wall_piece(real(d, pos[d] - t), s)
        zcopy(d, t - 1, s, piece, piece).wait_recv()

        @pl.when(pos[d] < nz - 1)
        def _():
            zcopy(d, t, s, piece, piece).start()

    for t in range(1, nz):
        @pl.loop(0, pieces)
        def _(s):
            if t == 1:
                gather_piece(s)

            @pl.when(s == 0)
            def _():
                for d in range(2):
                    @pl.when(t > pos[d])
                    def _():
                        turn_acts(real(d, nz - t + pos[d]), d)

            for d in range(2):
                @pl.when(t <= pos[d])
                def _():
                    pass_weight(d, t, s)

                @pl.when(t > pos[d])
                def _():
                    forward_sum(d, t, s)

            if t == 1:
                @pl.when(s == pieces - 1)
                def _():
                    input_grad(z)
            else:
                for d in range(2):
                    @pl.when((s == d) & (t - 1 <= pos[d]))
                    def _():
                        input_grad(real(d, pos[d] - (t - 1)))

    for d in range(2):
        @pl.when(nz - 1 <= pos[d])
        def _():
            input_grad(real(d, pos[d] - (nz - 1)))

    turn_acts(z, 0)

    @pl.loop(0, pieces)
    def _(s):
        own[:, part(s, pw)] = weight_piece(0, s)

    own_p = pltpu.make_async_copy(own, pz_out, l_sem.at[0])
    own_p.start()
    for d in range(2):
        @pl.when(pos[d] == 0)
        def _():
            rr[d, 0] = jnp.zeros((pieces, blk, pw), BF16)
            for s in range(pieces):
                fill = pltpu.make_async_copy(rr.at[d, 0, s], rs_out.at[d, :, part(s, pw)], l_sem.at[1])
                fill.start()
                fill.wait()

        @pl.when(pos[d] > 0)
        def _():
            for s in range(pieces):
                piece = rs_out.at[d, :, part(s, pw)]
                zcopy(d, nz - 1, s, piece, piece).wait_recv()

    pltpu.make_async_copy(ga_out, ga_out, ga_recv).wait()
    own_p.wait()
    for d in range(2):
        @pl.when(pos[d] < nz - 1)
        def _():
            for t in range(nz):
                @pl.loop(0, pieces)
                def _(s):
                    piece = sb.at[d, 0, s]
                    zcopy(d, t, s, piece, piece).wait_send()
    for k in range(3):
        @pl.loop(0, pieces)
        def _(s):
            gcopy(k, s, q, sib).wait_send()
    others = acts_l.at[pl.ds(0, total - tok)]
    pltpu.make_async_copy(others, others, a_send).wait()
    others = ga_s.at[pl.ds(0, total - tok)]
    pltpu.make_async_copy(others, others, ga_send).wait()


def per_device(acts, grad_out, proj_weight):
    ns = lax.axis_size("seq")
    nz = lax.axis_size("dp") // NQ
    tok, feats = acts.shape
    rg, cols = grad_out.shape
    blk = proj_weight.shape[0]
    total_tokens = tok * ns * nz * NQ
    pieces = min(8, cols // 128)
    total = NQ * rg
    anywhere = pl.BlockSpec(memory_space=pl.ANY)
    flops = 4 * total * nz * blk * cols
    parts, sums, own = pl.pallas_call(
        functools.partial(kernel, nz, ns, pieces),
        out_shape=(
            jax.ShapeDtypeStruct((ns, tok, feats), BF16),
            jax.ShapeDtypeStruct((2, blk, cols), BF16),
            jax.ShapeDtypeStruct((blk, cols), F32),
        ),
        in_specs=[anywhere] * 3,
        out_specs=(anywhere,) * 3,
        scratch_shapes=[
            pltpu.VMEM((total, cols), BF16),
            pltpu.VMEM((total, nz * blk), BF16),
            pltpu.VMEM((nz * blk, cols), BF16),
            pltpu.VMEM((total, nz * blk), BF16),
            pltpu.VMEM((2, blk, total), BF16),
            pltpu.VMEM((2, nz - 1, pieces, blk, cols // pieces), BF16),
            pltpu.VMEM((2, nz - 1, pieces, blk, cols // pieces), BF16),
            pltpu.VMEM((2, blk, cols // pieces), F32),
            pltpu.VMEM((blk, cols), F32),
            pltpu.SemaphoreType.DMA((3, pieces)),
            pltpu.SemaphoreType.DMA((3, pieces)),
            pltpu.SemaphoreType.DMA,
            pltpu.SemaphoreType.DMA((nz,)),
            pltpu.SemaphoreType.DMA,
            pltpu.SemaphoreType.DMA,
            pltpu.SemaphoreType.DMA((2, nz, pieces)),
            pltpu.SemaphoreType.DMA((2, nz, pieces)),
            pltpu.SemaphoreType.DMA((2,)),
        ],
        compiler_params=pltpu.CompilerParams(
            collective_id=0, has_side_effects=True, vmem_limit_bytes=40 * 1024 * 1024),
        cost_estimate=pl.CostEstimate(flops=flops, bytes_accessed=16 * 1024 * 1024, transcendentals=0),
    )(*[pltpu.with_memory_space_constraint(a, pltpu.HBM) for a in (acts, grad_out, proj_weight)])
    grad_acts = jnp.sum(parts.astype(F32), axis=0)
    summed = own + sums[0].astype(F32) + sums[1].astype(F32)
    grad_weight = summed / jnp.sqrt(jnp.float32(total_tokens))
    return (grad_acts, grad_weight)


def solution(mesh):
    in_specs = (P(("dp", "seq"), None), P("dp", "seq"), P("dp", "seq"))
    out_specs = (P(("dp", "seq"), None), P("dp", "seq"))
    return jax.shard_map(
        per_device, mesh=mesh, in_specs=in_specs, out_specs=out_specs, check_vma=False
    )
```

```python
import functools

import jax
import jax.numpy as jnp
from jax import lax
from jax.experimental import pallas as pl
from jax.experimental.pallas import tpu as pltpu
from jax.sharding import PartitionSpec as P

MESH = pl.DeviceIdType.MESH
NQ = 4
BF16 = jnp.bfloat16
F32 = jnp.float32


def kernel(nz, ns, pieces, acts, go, w, ga_out, rs_out, pz_out, go_l, acts_l, wall, ga_s,
           acts_t, rr, sb, pbuf, own, go_send, go_recv, a_send, a_recv, ga_send, ga_recv,
           z_send, z_recv, l_sem):
    tok = acts.shape[0]
    rg, cols = go.shape
    blk = w.shape[0]
    h = blk // pieces
    pw = cols // pieces
    total = NQ * rg
    dp = lax.axis_index("dp")
    x = lax.axis_index("seq")
    z = dp // NQ
    q = dp % NQ
    mirror = nz - 1 - z
    pos = (z, mirror)

    def real(d, i):
        return i if d == 0 else nz - 1 - i

    def layer(qq, xx):
        return {"dp": z * NQ + qq, "seq": xx}

    def ahead(d):
        return {"dp": (z + (1 if d == 0 else -1)) * NQ + q, "seq": x}

    def part(i, size):
        return pl.ds(pl.multiple_of(i * size, size), size)

    barrier = pltpu.get_barrier_semaphore()
    for o in range(NQ * ns):
        @pl.when(o != q * ns + x)
        def _():
            pl.semaphore_signal(barrier, inc=1, device_id=layer(o // ns, o % ns), device_id_type=MESH)
    for d in range(2):
        @pl.when(pos[d] < nz - 1)
        def _():
            pl.semaphore_signal(barrier, inc=1, device_id=ahead(d), device_id_type=MESH)
    beside = (z + nz - 1) // nz + (mirror + nz - 1) // nz
    pl.semaphore_wait(barrier, NQ * ns - 1 + beside)

    def zcopy(d, t, s, src, dst):
        return pltpu.make_async_remote_copy(
            src_ref=src, dst_ref=dst, send_sem=z_send.at[d, t, s], recv_sem=z_recv.at[d, t, s],
            device_id=ahead(d), device_id_type=MESH)

    def wall_piece(i, s):
        return wall.at[pl.ds(pl.multiple_of(i * blk + s * h, h), h)]

    def send_weight(s):
        for d in range(2):
            @pl.when(pos[d] < nz - 1)
            def _():
                zcopy(d, 0, s, w.at[part(s, h)], wall_piece(z, s)).start()

    sib = q + 1 - 2 * (q % 2)
    far = (q + 2) % NQ
    sibfar = (sib + 2) % NQ

    def gcopy(k, s, slot, target):
        src = go.at[:, part(s, pw)] if k < 2 else go_l.at[part(slot, rg), part(s, pw)]
        return pltpu.make_async_remote_copy(
            src_ref=src, dst_ref=go_l.at[part(slot, rg), part(s, pw)], send_sem=go_send.at[k, s],
            recv_sem=go_recv.at[k, s], device_id=layer(target, x), device_id_type=MESH)

    def send_acts(m):
        @pl.loop(0, NQ * ns)
        def _(o):
            qq, xx = o // ns, o % ns
            src = acts.at[:, part(m * NQ + qq, blk)]
            dst = acts_l.at[part(q * ns + x, tok), part(m, blk)]

            @pl.when(o == q * ns + x)
            def _():
                pltpu.make_async_copy(src, dst, a_recv.at[m]).start()

            @pl.when(o != q * ns + x)
            def _():
                pltpu.make_async_remote_copy(
                    src_ref=src, dst_ref=dst, send_sem=a_send, recv_sem=a_recv.at[m],
                    device_id=layer(qq, xx), device_id_type=MESH).start()

    def send_acts_for(t):
        for d in range(2):
            @pl.when(t > pos[d])
            def _():
                send_acts(real(d, nz - t + pos[d]))

    gcopy(1, 0, q, far).start()
    gcopy(0, 0, q, sib).start()
    send_weight(0)
    send_acts_for(1)
    send_weight(1)
    gcopy(1, 1, q, far).start()
    gcopy(0, 1, q, sib).start()
    own_go = pltpu.make_async_copy(go, go_l.at[part(q, rg)], l_sem.at[0])
    own_go.start()
    own_w = pltpu.make_async_copy(w, wall.at[part(z, blk)], l_sem.at[1])
    own_w.start()

    def gather_piece(s):
        gcopy(1, s, far, far).wait_recv()

        gcopy(2, s, far, sib).start()

        @pl.when(s + 2 < pieces)
        def _():
            gcopy(1, s + 2, q, far).start()
            gcopy(0, s + 2, q, sib).start()
            send_weight(s + 2)

        @pl.when(s == pieces - 2)
        def _():
            send_acts_for(2)

        @pl.when(s == pieces - 1)
        def _():
            for t in range(3, nz):
                send_acts_for(t)
            send_acts(z)

        gcopy(0, s, sib, sib).wait_recv()
        gcopy(2, s, sibfar, sib).wait_recv()

        @pl.when(s == 0)
        def _():
            own_go.wait()
            own_w.wait()

    def input_grad(m):
        @pl.loop(0, NQ)
        def _(qq):
            out = lax.dot_general(
                go_l[part(qq, rg), :], wall[part(m, blk), :], (((1,), (1,)), ((), ())),
                preferred_element_type=F32)
            ga_s[part(qq, rg), part(m, blk)] = out.astype(BF16)

            @pl.loop(0, ns)
            def _(xx):
                src = ga_s.at[part(qq * ns + xx, tok), part(m, blk)]
                dst = ga_out.at[x, :, part(m * NQ + q, blk)]
                mine = (qq * ns + xx) == (q * ns + x)

                @pl.when(mine)
                def _():
                    pltpu.make_async_copy(src, dst, ga_recv).start()

                @pl.when(jnp.logical_not(mine))
                def _():
                    pltpu.make_async_remote_copy(
                        src_ref=src, dst_ref=dst, send_sem=ga_send, recv_sem=ga_recv,
                        device_id=layer(qq, xx), device_id_type=MESH).start()

    def turn_acts(m, slot):
        block = acts_l.at[:, part(m, blk)]
        pltpu.make_async_copy(block, block, a_recv.at[m]).wait()
        acts_t[slot] = acts_l[:, part(m, blk)].T

    def weight_piece(slot, s):
        return jnp.dot(acts_t[slot], go_l[:, part(s, pw)], preferred_element_type=F32)

    step = min(blk, 64)

    def forward_sum(d, t, s):
        pbuf[d] = weight_piece(d, s)

        def emit(add):
            @pl.loop(0, blk // step)
            def _(i):
                r = part(i, step)
                value = pbuf[d, r, :]
                if add:
                    value = value + rr[d, t - 1, s, r, :].astype(F32)
                sb[d, t - 1, s, r, :] = value.astype(BF16)

        @pl.when(pos[d] > 0)
        def _():
            piece = rr.at[d, t - 1, s]
            zcopy(d, t - 1, s, piece, piece).wait_recv()
            emit(True)

        @pl.when(pos[d] == 0)
        def _():
            emit(False)

        dst = rs_out.at[d, :, part(s, pw)] if t == nz - 1 else rr.at[d, t, s]
        zcopy(d, t, s, sb.at[d, t - 1, s], dst).start()

    def pass_weight(d, t, s):
        piece = wall_piece(real(d, pos[d] - t), s)
        zcopy(d, t - 1, s, piece, piece).wait_recv()

        @pl.when(pos[d] < nz - 1)
        def _():
            zcopy(d, t, s, piece, piece).start()

    for t in range(1, nz):
        @pl.loop(0, pieces)
        def _(s):
            if t == 1:
                gather_piece(s)

            @pl.when(s == 0)
            def _():
                for d in range(2):
                    @pl.when(t > pos[d])
                    def _():
                        turn_acts(real(d, nz - t + pos[d]), d)

            for d in range(2):
                @pl.when(t <= pos[d])
                def _():
                    pass_weight(d, t, s)

                @pl.when(t > pos[d])
                def _():
                    forward_sum(d, t, s)

            if t == 1:
                @pl.when(s == pieces - 1)
                def _():
                    input_grad(z)
            else:
                for d in range(2):
                    @pl.when((s == d) & (t - 1 <= pos[d]))
                    def _():
                        input_grad(real(d, pos[d] - (t - 1)))

    for d in range(2):
        @pl.when(nz - 1 <= pos[d])
        def _():
            input_grad(real(d, pos[d] - (nz - 1)))

    turn_acts(z, 0)

    @pl.loop(0, pieces)
    def _(s):
        own[:, part(s, pw)] = weight_piece(0, s)

    own_p = pltpu.make_async_copy(own, pz_out, l_sem.at[0])
    own_p.start()
    for d in range(2):
        @pl.when(pos[d] == 0)
        def _():
            rr[d, 0] = jnp.zeros((pieces, blk, pw), BF16)
            for s in range(pieces):
                fill = pltpu.make_async_copy(rr.at[d, 0, s], rs_out.at[d, :, part(s, pw)], l_sem.at[1])
                fill.start()
                fill.wait()

        @pl.when(pos[d] > 0)
        def _():
            for s in range(pieces):
                piece = rs_out.at[d, :, part(s, pw)]
                zcopy(d, nz - 1, s, piece, piece).wait_recv()

    pltpu.make_async_copy(ga_out, ga_out, ga_recv).wait()
    own_p.wait()
    for d in range(2):
        @pl.when(pos[d] < nz - 1)
        def _():
            for t in range(nz):
                @pl.loop(0, pieces)
                def _(s):
                    piece = sb.at[d, 0, s]
                    zcopy(d, t, s, piece, piece).wait_send()
    for k in range(3):
        @pl.loop(0, pieces)
        def _(s):
            gcopy(k, s, q, sib).wait_send()
    others = acts_l.at[pl.ds(0, total - tok)]
    pltpu.make_async_copy(others, others, a_send).wait()
    others = ga_s.at[pl.ds(0, total - tok)]
    pltpu.make_async_copy(others, others, ga_send).wait()


def per_device(acts, grad_out, proj_weight):
    ns = lax.axis_size("seq")
    nz = lax.axis_size("dp") // NQ
    tok, feats = acts.shape
    rg, cols = grad_out.shape
    blk = proj_weight.shape[0]
    total_tokens = tok * ns * nz * NQ
    pieces = min(2, cols // 128)
    total = NQ * rg
    anywhere = pl.BlockSpec(memory_space=pl.ANY)
    flops = 4 * total * nz * blk * cols
    parts, sums, own = pl.pallas_call(
        functools.partial(kernel, nz, ns, pieces),
        out_shape=(
            jax.ShapeDtypeStruct((ns, tok, feats), BF16),
            jax.ShapeDtypeStruct((2, blk, cols), BF16),
            jax.ShapeDtypeStruct((blk, cols), F32),
        ),
        in_specs=[anywhere] * 3,
        out_specs=(anywhere,) * 3,
        scratch_shapes=[
            pltpu.VMEM((total, cols), BF16),
            pltpu.VMEM((total, nz * blk), BF16),
            pltpu.VMEM((nz * blk, cols), BF16),
            pltpu.VMEM((total, nz * blk), BF16),
            pltpu.VMEM((2, blk, total), BF16),
            pltpu.VMEM((2, nz - 1, pieces, blk, cols // pieces), BF16),
            pltpu.VMEM((2, nz - 1, pieces, blk, cols // pieces), BF16),
            pltpu.VMEM((2, blk, cols // pieces), F32),
            pltpu.VMEM((blk, cols), F32),
            pltpu.SemaphoreType.DMA((3, pieces)),
            pltpu.SemaphoreType.DMA((3, pieces)),
            pltpu.SemaphoreType.DMA,
            pltpu.SemaphoreType.DMA((nz,)),
            pltpu.SemaphoreType.DMA,
            pltpu.SemaphoreType.DMA,
            pltpu.SemaphoreType.DMA((2, nz, pieces)),
            pltpu.SemaphoreType.DMA((2, nz, pieces)),
            pltpu.SemaphoreType.DMA((2,)),
        ],
        compiler_params=pltpu.CompilerParams(
            collective_id=0, has_side_effects=True, vmem_limit_bytes=40 * 1024 * 1024),
        cost_estimate=pl.CostEstimate(flops=flops, bytes_accessed=16 * 1024 * 1024, transcendentals=0),
    )(*[pltpu.with_memory_space_constraint(a, pltpu.HBM) for a in (acts, grad_out, proj_weight)])
    grad_acts = jnp.sum(parts.astype(F32), axis=0)
    summed = own + sums[0].astype(F32) + sums[1].astype(F32)
    grad_weight = summed / jnp.sqrt(jnp.float32(total_tokens))
    return (grad_acts, grad_weight)


def solution(mesh):
    in_specs = (P(("dp", "seq"), None), P("dp", "seq"), P("dp", "seq"))
    out_specs = (P(("dp", "seq"), None), P("dp", "seq"))
    return jax.shard_map(
        per_device, mesh=mesh, in_specs=in_specs, out_specs=out_specs, check_vma=False
    )
```

```python
import functools

import jax
import jax.numpy as jnp
import numpy as np
from jax import lax
from jax.experimental import pallas as pl
from jax.experimental.pallas import tpu as pltpu
from jax.sharding import PartitionSpec as P

MESH = pl.DeviceIdType.MESH
NQ = 4
BF16 = jnp.bfloat16
F32 = jnp.float32


def kernel(nz, ns, pieces, acts, go, w, ga_out, rs_out, pz_out, go_l, acts_l, wall, ga_s,
           acts_t, rr, sb, pbuf, own, go_send, go_recv, a_send, a_recv, ga_send, ga_recv,
           z_send, z_recv, l_sem):
    tok = acts.shape[0]
    rg, cols = go.shape
    blk = w.shape[0]
    h = blk // pieces
    pw = cols // pieces
    total = NQ * rg
    dp = lax.axis_index("dp")
    x = lax.axis_index("seq")
    z = dp // NQ
    q = dp % NQ
    mirror = nz - 1 - z
    pos = (z, mirror)

    def real(d, i):
        return i if d == 0 else nz - 1 - i

    def layer(qq, xx):
        return {"dp": z * NQ + qq, "seq": xx}

    def ahead(d):
        return {"dp": (z + (1 if d == 0 else -1)) * NQ + q, "seq": x}

    def part(i, size):
        return pl.ds(pl.multiple_of(i * size, size), size)

    barrier = pltpu.get_barrier_semaphore()
    for o in range(NQ * ns):
        @pl.when(o != q * ns + x)
        def _():
            pl.semaphore_signal(barrier, inc=1, device_id=layer(o // ns, o % ns), device_id_type=MESH)
    for d in range(2):
        @pl.when(pos[d] < nz - 1)
        def _():
            pl.semaphore_signal(barrier, inc=1, device_id=ahead(d), device_id_type=MESH)
    beside = (z + nz - 1) // nz + (mirror + nz - 1) // nz
    pl.semaphore_wait(barrier, NQ * ns - 1 + beside)

    def zcopy(d, t, s, src, dst):
        return pltpu.make_async_remote_copy(
            src_ref=src, dst_ref=dst, send_sem=z_send.at[d, t, s], recv_sem=z_recv.at[d, t, s],
            device_id=ahead(d), device_id_type=MESH)

    def wall_piece(i, s):
        return wall.at[pl.ds(pl.multiple_of(i * blk + s * h, h), h)]

    def send_weight(s):
        for d in range(2):
            @pl.when(pos[d] < nz - 1)
            def _():
                zcopy(d, 0, s, w.at[part(s, h)], wall_piece(z, s)).start()

    sib = q + 1 - 2 * (q % 2)
    far = (q + 2) % NQ
    sibfar = (sib + 2) % NQ

    def gcopy(k, s, slot, target):
        src = go.at[:, part(s, pw)] if k < 2 else go_l.at[part(slot, rg), part(s, pw)]
        return pltpu.make_async_remote_copy(
            src_ref=src, dst_ref=go_l.at[part(slot, rg), part(s, pw)], send_sem=go_send.at[k, s],
            recv_sem=go_recv.at[k, s], device_id=layer(target, x), device_id_type=MESH)

    def send_acts(m):
        @pl.loop(0, NQ * ns)
        def _(o):
            qq, xx = o // ns, o % ns
            src = acts.at[:, part(m * NQ + qq, blk)]
            dst = acts_l.at[part(q * ns + x, tok), part(m, blk)]

            @pl.when(o == q * ns + x)
            def _():
                pltpu.make_async_copy(src, dst, a_recv.at[m]).start()

            @pl.when(o != q * ns + x)
            def _():
                pltpu.make_async_remote_copy(
                    src_ref=src, dst_ref=dst, send_sem=a_send, recv_sem=a_recv.at[m],
                    device_id=layer(qq, xx), device_id_type=MESH).start()

    def send_acts_for(t):
        for d in range(2):
            @pl.when(t > pos[d])
            def _():
                send_acts(real(d, nz - t + pos[d]))

    gcopy(1, 0, q, far).start()
    gcopy(0, 0, q, sib).start()
    send_weight(0)
    send_acts_for(1)
    send_weight(1)
    gcopy(1, 1, q, far).start()
    gcopy(0, 1, q, sib).start()
    own_go = pltpu.make_async_copy(go, go_l.at[part(q, rg)], l_sem.at[0])
    own_go.start()
    own_w = pltpu.make_async_copy(w, wall.at[part(z, blk)], l_sem.at[1])
    own_w.start()

    def gather_piece(s):
        gcopy(1, s, far, far).wait_recv()

        gcopy(2, s, far, sib).start()

        @pl.when(s + 2 < pieces)
        def _():
            gcopy(1, s + 2, q, far).start()
            gcopy(0, s + 2, q, sib).start()
            send_weight(s + 2)

        @pl.when(s == pieces - 2)
        def _():
            send_acts_for(2)

        @pl.when(s == pieces - 1)
        def _():
            for t in range(3, nz):
                send_acts_for(t)
            send_acts(z)

        gcopy(0, s, sib, sib).wait_recv()
        gcopy(2, s, sibfar, sib).wait_recv()

        @pl.when(s == 0)
        def _():
            own_go.wait()
            own_w.wait()

    def input_grad(m):
        @pl.loop(0, NQ)
        def _(qq):
            out = lax.dot_general(
                go_l[part(qq, rg), :], wall[part(m, blk), :], (((1,), (1,)), ((), ())),
                preferred_element_type=F32)
            ga_s[part(qq, rg), part(m, blk)] = out.astype(BF16)

            @pl.loop(0, ns)
            def _(xx):
                src = ga_s.at[part(qq * ns + xx, tok), part(m, blk)]
                dst = ga_out.at[x, :, part(m * NQ + q, blk)]
                mine = (qq * ns + xx) == (q * ns + x)

                @pl.when(mine)
                def _():
                    pltpu.make_async_copy(src, dst, ga_recv).start()

                @pl.when(jnp.logical_not(mine))
                def _():
                    pltpu.make_async_remote_copy(
                        src_ref=src, dst_ref=dst, send_sem=ga_send, recv_sem=ga_recv,
                        device_id=layer(qq, xx), device_id_type=MESH).start()

    def turn_acts(m, slot):
        block = acts_l.at[:, part(m, blk)]
        pltpu.make_async_copy(block, block, a_recv.at[m]).wait()
        acts_t[slot] = acts_l[:, part(m, blk)].T

    def weight_piece(slot, s):
        return jnp.dot(acts_t[slot], go_l[:, part(s, pw)], preferred_element_type=F32)

    step = min(blk, 64)

    def forward_sum(d, t, s):
        pbuf[d] = weight_piece(d, s)

        def emit(add):
            @pl.loop(0, blk // step)
            def _(i):
                r = part(i, step)
                value = pbuf[d, r, :]
                if add:
                    value = value + rr[d, t - 1, s, r, :].astype(F32)
                sb[d, t - 1, s, r, :] = value.astype(BF16)

        @pl.when(pos[d] > 0)
        def _():
            piece = rr.at[d, t - 1, s]
            zcopy(d, t - 1, s, piece, piece).wait_recv()
            emit(True)

        @pl.when(pos[d] == 0)
        def _():
            emit(False)

        dst = rs_out.at[d, :, part(s, pw)] if t == nz - 1 else rr.at[d, t, s]
        zcopy(d, t, s, sb.at[d, t - 1, s], dst).start()

    def pass_weight(d, t, s):
        piece = wall_piece(real(d, pos[d] - t), s)
        zcopy(d, t - 1, s, piece, piece).wait_recv()

        @pl.when(pos[d] < nz - 1)
        def _():
            zcopy(d, t, s, piece, piece).start()

    for t in range(1, nz):
        @pl.loop(0, pieces)
        def _(s):
            if t == 1:
                gather_piece(s)

            @pl.when(s == 0)
            def _():
                for d in range(2):
                    @pl.when(t > pos[d])
                    def _():
                        turn_acts(real(d, nz - t + pos[d]), d)

            for d in range(2):
                @pl.when(t <= pos[d])
                def _():
                    pass_weight(d, t, s)

                @pl.when(t > pos[d])
                def _():
                    forward_sum(d, t, s)

            if t == 1:
                @pl.when(s == pieces - 1)
                def _():
                    input_grad(z)
            else:
                for d in range(2):
                    @pl.when((s == d) & (t - 1 <= pos[d]))
                    def _():
                        input_grad(real(d, pos[d] - (t - 1)))

    for d in range(2):
        @pl.when(nz - 1 <= pos[d])
        def _():
            input_grad(real(d, pos[d] - (nz - 1)))

    turn_acts(z, 0)

    @pl.loop(0, pieces)
    def _(s):
        own[:, part(s, pw)] = weight_piece(0, s)

    own_p = pltpu.make_async_copy(own, pz_out, l_sem.at[0])
    own_p.start()
    for d in range(2):
        @pl.when(pos[d] == 0)
        def _():
            rr[d, 0] = jnp.zeros((pieces, blk, pw), BF16)
            for s in range(pieces):
                fill = pltpu.make_async_copy(rr.at[d, 0, s], rs_out.at[d, :, part(s, pw)], l_sem.at[1])
                fill.start()
                fill.wait()

        @pl.when(pos[d] > 0)
        def _():
            for s in range(pieces):
                piece = rs_out.at[d, :, part(s, pw)]
                zcopy(d, nz - 1, s, piece, piece).wait_recv()

    pltpu.make_async_copy(ga_out, ga_out, ga_recv).wait()
    own_p.wait()
    for d in range(2):
        @pl.when(pos[d] < nz - 1)
        def _():
            for t in range(nz):
                @pl.loop(0, pieces)
                def _(s):
                    piece = sb.at[d, 0, s]
                    zcopy(d, t, s, piece, piece).wait_send()
    for k in range(3):
        @pl.loop(0, pieces)
        def _(s):
            gcopy(k, s, q, sib).wait_send()
    others = acts_l.at[pl.ds(0, total - tok)]
    pltpu.make_async_copy(others, others, a_send).wait()
    others = ga_s.at[pl.ds(0, total - tok)]
    pltpu.make_async_copy(others, others, ga_send).wait()


def finish(ns, root, parts, sums, own, ga, gw, ga_buf, gw_buf, sem):
    def emit(out, buf, k, step, value):
        @pl.loop(0, buf.shape[0] // step)
        def _(i):
            r = pl.ds(pl.multiple_of(i * step, step), step)
            buf[r, :] = value(r)
            pltpu.make_async_copy(buf.at[r], out.at[r], sem.at[k]).start()

    def added(r):
        value = parts[0, r, :].astype(F32)
        for j in range(1, ns):
            value = value + parts[j, r, :].astype(F32)
        return value

    emit(ga, ga_buf, 0, 16, added)
    emit(gw, gw_buf, 1, 32,
         lambda r: (own[r, :] + sums[0, r, :].astype(F32) + sums[1, r, :].astype(F32)) / root)
    pltpu.make_async_copy(ga_buf, ga, sem.at[0]).wait()
    pltpu.make_async_copy(gw_buf, gw, sem.at[1]).wait()


def per_device(acts, grad_out, proj_weight):
    ns = lax.axis_size("seq")
    nz = lax.axis_size("dp") // NQ
    tok, feats = acts.shape
    rg, cols = grad_out.shape
    blk = proj_weight.shape[0]
    total_tokens = tok * ns * nz * NQ
    pieces = min(2, cols // 128)
    total = NQ * rg
    anywhere = pl.BlockSpec(memory_space=pl.ANY)
    flops = 4 * total * nz * blk * cols
    parts, sums, own = pl.pallas_call(
        functools.partial(kernel, nz, ns, pieces),
        out_shape=(
            jax.ShapeDtypeStruct((ns, tok, feats), BF16),
            jax.ShapeDtypeStruct((2, blk, cols), BF16),
            jax.ShapeDtypeStruct((blk, cols), F32),
        ),
        in_specs=[anywhere] * 3,
        out_specs=(anywhere,) * 3,
        scratch_shapes=[
            pltpu.VMEM((total, cols), BF16),
            pltpu.VMEM((total, nz * blk), BF16),
            pltpu.VMEM((nz * blk, cols), BF16),
            pltpu.VMEM((total, nz * blk), BF16),
            pltpu.VMEM((2, blk, total), BF16),
            pltpu.VMEM((2, nz - 1, pieces, blk, cols // pieces), BF16),
            pltpu.VMEM((2, nz - 1, pieces, blk, cols // pieces), BF16),
            pltpu.VMEM((2, blk, cols // pieces), F32),
            pltpu.VMEM((blk, cols), F32),
            pltpu.SemaphoreType.DMA((3, pieces)),
            pltpu.SemaphoreType.DMA((3, pieces)),
            pltpu.SemaphoreType.DMA,
            pltpu.SemaphoreType.DMA((nz,)),
            pltpu.SemaphoreType.DMA,
            pltpu.SemaphoreType.DMA,
            pltpu.SemaphoreType.DMA((2, nz, pieces)),
            pltpu.SemaphoreType.DMA((2, nz, pieces)),
            pltpu.SemaphoreType.DMA((2,)),
        ],
        compiler_params=pltpu.CompilerParams(
            collective_id=0, has_side_effects=True, vmem_limit_bytes=40 * 1024 * 1024),
        cost_estimate=pl.CostEstimate(flops=flops, bytes_accessed=16 * 1024 * 1024, transcendentals=0),
    )(*[pltpu.with_memory_space_constraint(a, pltpu.HBM) for a in (acts, grad_out, proj_weight)])
    root = np.sqrt(np.float32(total_tokens))
    shapes = ((tok, feats), (blk, cols))
    return pl.pallas_call(
        functools.partial(finish, ns, root),
        out_shape=tuple(jax.ShapeDtypeStruct(shape, F32) for shape in shapes),
        in_specs=[pl.BlockSpec(memory_space=pltpu.VMEM)] * 3,
        out_specs=(anywhere,) * 2,
        scratch_shapes=[pltpu.VMEM(shape, F32) for shape in shapes] + [pltpu.SemaphoreType.DMA((2,))],
        compiler_params=pltpu.CompilerParams(vmem_limit_bytes=40 * 1024 * 1024),
    )(parts, sums, own)


def solution(mesh):
    in_specs = (P(("dp", "seq"), None), P("dp", "seq"), P("dp", "seq"))
    out_specs = (P(("dp", "seq"), None), P("dp", "seq"))
    return jax.shard_map(
        per_device, mesh=mesh, in_specs=in_specs, out_specs=out_specs, check_vma=False
    )
```
